512 devices in a mesh: row: 32 (over z_hi, x, core), col: 16 (over y, z_lo).
Axes of the slice: x: 4, y: 8, z: 8 (z_hi: 4, z_lo: 2; z = z_hi * 2 + z_lo), core: 2. Of those that a mesh axis runs over, the one named last changes fastest.
Arguments:
- pair: float32 [384, 384, 128], P('row', 'col'), may hold values from -6 to 6
- cotangent: float32 [384, 384, 128], P('row', 'col'), may hold values from -6 to 6
- norm_gain: float32 [128], replicated, may hold values from 0.5 to 1.5
- gate_a: float32 [128, 128], replicated, may hold values from -0.5 to 0.5
- proj_a: float32 [128, 128], replicated, may hold values from -0.5 to 0.5
- gate_b: float32 [128, 128], replicated, may hold values from -0.5 to 0.5
- proj_b: float32 [128, 128], replicated, may hold values from -0.5 to 0.5
- mix_gain: float32 [128], replicated, may hold values from 0.5 to 1.5
- out_gate: float32 [128, 128], replicated, may hold values from -0.5 to 0.5
- out_proj: float32 [128, 128], replicated, may hold values from -0.5 to 0.5
Outputs:
- pair_grad: float32 [384, 384, 128], P('row', 'col')
The draws below stay inside these ranges and needn't reach their ends.
All inputs are finite; a program needn't handle non-finite values.
Results may differ from the reference program's by a relative error of at most 0.000084.
Values sent between devices are 32-bit elements; how exact they have to be, the bound alone decides.
A program may use at most 64 MiB of HBM per device.

```python
import jax
import jax.numpy as jnp
from jax import lax

C = 128
H = 128
RES = 384


def block_scale(rng, extent, split, least, top_value):
    def one(axis_at, parts):
        heights = jax.random.uniform(jax.random.fold_in(jax.random.fold_in(rng, 6), axis_at), (parts,), jnp.float32, least / len(split), top_value / len(split))
        return jnp.repeat(jnp.exp(heights), extent[axis_at] // parts).reshape((-1,) + (1,) * (len(extent) - axis_at - 1))

    level = one(*split[0])
    for cut in split[1:]:
        level = level * one(*cut)
    return level


def scatter_about(own_key, dims, width, most, cuts=(), held_as=jnp.bfloat16):
    level = block_scale(own_key, dims, cuts, -0.22, 0.18) if cuts else 1.0
    result = jax.random.normal(own_key, dims, jnp.float32) * width * level
    return jnp.minimum(jnp.maximum(result, -most), most).astype(held_as)


def setup_inputs(seed: int = 0) -> dict:
    keys = jax.random.split(jax.random.key(seed), 11)
    pair = scatter_about(keys[0], (RES, RES, C), 1.0, 6.0, ((0, 32), (1, 16)), jnp.float32)
    cotangent = scatter_about(keys[1], (RES, RES, C), 1.0, 6.0, ((0, 32), (1, 16)), jnp.float32)
    norm_gain = jnp.clip(jax.random.uniform(keys[2], (C,), jnp.float32, 0.5, 1.5), 0.5, 1.5)
    gate_a = scatter_about(keys[3], (C, H), C ** -0.5, 0.5, (), jnp.float32)
    proj_a = scatter_about(keys[4], (C, H), C ** -0.5, 0.5, (), jnp.float32)
    gate_b = scatter_about(keys[5], (C, H), C ** -0.5, 0.5, (), jnp.float32)
    proj_b = scatter_about(keys[6], (C, H), C ** -0.5, 0.5, (), jnp.float32)
    mix_gain = jnp.clip(jax.random.uniform(keys[7], (H,), jnp.float32, 0.5, 1.5), 0.5, 1.5)
    out_gate = scatter_about(keys[8], (C, C), C ** -0.5, 0.5, (), jnp.float32)
    out_proj = scatter_about(keys[9], (H, C), H ** -0.5, 0.5, (), jnp.float32)
    return {"pair": pair, "cotangent": cotangent, "norm_gain": norm_gain, "gate_a": gate_a, "proj_a": proj_a, "gate_b": gate_b, "proj_b": proj_b, "mix_gain": mix_gain, "out_gate": out_gate, "out_proj": out_proj}


def layer_norm(values, gain):
    centred = values - lax.optimization_barrier(jnp.mean(values, axis=-1, keepdims=True))
    variance = lax.optimization_barrier(jnp.mean(centred * centred, axis=-1, keepdims=True))
    return centred * lax.rsqrt(variance + 1e-05) * gain

def forward(pair, norm_gain, gate_a, proj_a, gate_b, proj_b, mix_gain, out_gate, out_proj):
    high = lax.Precision.HIGHEST
    normed = layer_norm(pair, norm_gain)
    left = jax.nn.sigmoid(jnp.einsum('ijc,ch->ijh', normed, gate_a, precision=high)) * jnp.einsum('ijc,ch->ijh', normed, proj_a, precision=high)
    right = jax.nn.sigmoid(jnp.einsum('ijc,ch->ijh', normed, gate_b, precision=high)) * jnp.einsum('ijc,ch->ijh', normed, proj_b, precision=high)
    mixed = jnp.einsum('ikh,jkh->ijh', left, right, precision=high)
    mixed_normed = layer_norm(mixed, mix_gain)
    gate = jax.nn.sigmoid(jnp.einsum('ijc,cd->ijd', normed, out_gate, precision=high))
    return gate * jnp.einsum('ijh,hc->ijc', mixed_normed, out_proj, precision=high)

def reference(pair, cotangent, norm_gain, gate_a, proj_a, gate_b, proj_b, mix_gain, out_gate, out_proj):

    def update(values):
        return forward(values, norm_gain, gate_a, proj_a, gate_b, proj_b, mix_gain, out_gate, out_proj)
    output, pullback = jax.vjp(update, pair)
    return pullback(cotangent)[0]
```

```python
import jax
import jax.numpy as jnp
from jax import lax
from jax.experimental import pallas as pl
from jax.experimental.pallas import tpu as pltpu
from jax.sharding import PartitionSpec as P

MESH = pl.DeviceIdType.MESH
F32 = jnp.float32
NN = (((1,), (0,)), ((), ()))
NT = (((1,), (1,)), ((), ()))


def split(values):
    high = values.astype(jnp.bfloat16)
    return high, (values - high.astype(F32)).astype(jnp.bfloat16)


def product(a, b, dims=NN):
    def one(x, y):
        return lax.dot_general(x, y, dims, preferred_element_type=F32)

    return one(a[0], b[1]) + one(a[1], b[0]) + one(a[0], b[0])


def column(ref):
    return jnp.broadcast_to(ref[...], (8, 128)).T[:, 0:1]


def mean0(values):
    return jnp.mean(values, axis=0, keepdims=True)


def kernel(pair_ref, cot_ref, norm_gain_ref, gate_a_ref, proj_a_ref, gate_b_ref, proj_b_ref, mix_gain_ref,
           out_gate_ref, out_proj_ref, out_ref,
           s1, r1, left_x, right_t, right_x, s2, r2, s3, r3, grad_x, dl_out, dl_in, dl_own, dr_full, dr_t, dr_in,
           s4, r4, keep, stats, send_sem, recv_sem, hop):
    row = lax.axis_index("row")
    col = lax.axis_index("col")
    core = row % 2
    low = (row // 2) % 2
    part = row // 4
    quarter = row % 4
    mine = col * 8 + part
    x_peer = (row + 2 - 4 * low, col)
    core_peer = (row + 1 - 2 * core, col)

    barrier = pltpu.get_barrier_semaphore()

    def signal(sem, device):
        pl.semaphore_signal(sem, inc=1, device_id=device, device_id_type=MESH)

    def greet_col(k, carry):
        signal(barrier, (row, (col + k) % 16))
        return carry

    def greet_row(k, carry):
        signal(barrier, ((row + 4 * k) % 32, col))
        return carry

    def pass_on(k, carry):
        signal(hop, ((row + 4 * k) % 32, col))
        return carry

    lax.fori_loop(1, 16, greet_col, 0)
    lax.fori_loop(1, 8, greet_row, 0)
    signal(barrier, x_peer)
    signal(barrier, core_peer)

    def remote(src, dst, phase, device):
        return pltpu.make_async_remote_copy(
            src_ref=src, dst_ref=dst, send_sem=send_sem.at[phase], recv_sem=recv_sem.at[phase],
            device_id=device, device_id_type=MESH)

    def wait(ref, sem):
        pltpu.make_async_copy(ref, ref, sem).wait()

    ng = column(norm_gain_ref)
    mg = column(mix_gain_ref)
    pair = pair_ref[...].reshape(288, 128).T
    centred = pair - mean0(pair)
    inverse = lax.rsqrt(mean0(centred * centred) + 1e-05)
    plain = centred * inverse
    normed = split(plain * ng)
    weights = jnp.concatenate(
        [gate_a_ref[...], proj_a_ref[...], gate_b_ref[...], proj_b_ref[...], out_gate_ref[...]], axis=1)
    projected = product(split(weights.T), normed)
    left_gate = jax.nn.sigmoid(projected[0:128])
    left_value = projected[128:256]
    right_gate = jax.nn.sigmoid(projected[256:384])
    right_value = projected[384:512]
    s1[:, 0, :] = jnp.concatenate([left_gate * left_value, right_gate * right_value], axis=1)

    pl.semaphore_wait(barrier, 24)
    lax.fori_loop(1, 8, pass_on, 0)
    pl.semaphore_wait(hop, 7)

    def send_edges(k, carry):
        q = (mine + k) % 128
        remote(s1.at[q], r1.at[mine], 0, ((q % 8) * 4 + quarter, q // 8)).start()
        return carry

    lax.fori_loop(1, 128, send_edges, 0)
    pltpu.make_async_copy(s1.at[mine], r1.at[mine], recv_sem.at[0]).start()

    keep[0] = plain
    keep[1] = left_gate
    keep[2] = left_value * left_gate * (1.0 - left_gate)
    keep[3] = right_gate
    keep[4] = right_value * right_gate * (1.0 - right_gate)
    out_sig = jax.nn.sigmoid(projected[512:640])
    grad_value = cot_ref[...].reshape(288, 128).T * out_sig
    keep[5] = grad_value * (1.0 - out_sig)
    out_proj = out_proj_ref[...]
    scaled = product(split(out_proj), split(grad_value)) * mg
    keep[6] = scaled - mean0(scaled)
    keep[7] = scaled
    stats[0:1] = inverse

    wait(r1, recv_sem.at[0])
    for n in range(12):
        left_x[low, 8 * n:8 * n + 8, :] = jnp.concatenate(
            [r1[8 * c:8 * c + 8, 0, 24 * n:24 * n + 24] for c in range(16)], axis=1)
    send_left = remote(left_x.at[low], left_x.at[low], 1, x_peer)
    send_left.start()
    for n in range(12):
        right_t[core, 8 * n:8 * n + 8, :] = jnp.concatenate(
            [r1[8 * c:8 * c + 8, 0, 24 * n + 288:24 * n + 312] for c in range(16)], axis=1)
    send_right = remote(right_t.at[core], right_t.at[core], 2, core_peer)
    send_right.start()
    send_right.wait_recv()
    for side in range(2):
        for n in range(12):
            for t in range(3):
                right_x[t, pl.ds(12 * side + n, 8, stride=24), :] = right_t[
                    side, 8 * n:8 * n + 8, 128 * t:128 * t + 128]

    def right_all():
        return split(jnp.concatenate([right_x[t] for t in range(3)], axis=1))

    right = right_all()

    same = (col % 2) == low
    place = (col // 2) * 8 + part

    def mix(half):
        mixed = product(split(left_x[half]), right, NT)
        for b in range(8):
            s2[pl.ds(half * 64 + 8 * b, 8), 0, :] = jnp.concatenate(
                [mixed[8 * n:8 * n + 8, 24 * b:24 * b + 24] for n in range(12)], axis=1)

    def mixed_copy(half, q):
        target = ((q % 8) * 4 + half * 2 + core, (q // 8) * 2 + low)
        return remote(s2.at[half * 64 + q], r2.at[mine], 3, target)

    mix(low)

    def send_mixed_own(k, carry):
        mixed_copy(low, (place + k) % 64).start()
        return carry

    lax.fori_loop(1, 64, send_mixed_own, 0)

    @pl.when(same)
    def _():
        pltpu.make_async_copy(s2.at[low * 64 + place], r2.at[mine], recv_sem.at[3]).start()

    @pl.when(jnp.logical_not(same))
    def _():
        mixed_copy(low, place).start()

    send_left.wait_recv()
    mix(1 - low)

    def send_mixed_other(k, carry):
        mixed_copy(1 - low, (place + k) % 64).start()
        return carry

    lax.fori_loop(0, 64, send_mixed_other, 0)

    wait(r2, recv_sem.at[3])
    mixed = r2[:, 0, :]
    mixed = mixed - mean0(mixed)
    mixed_inverse = lax.rsqrt(mean0(mixed * mixed) + 1e-05)
    mixed_plain = mixed * mixed_inverse
    second = mean0(keep[7] * mixed_plain)
    s3[:, 0, :] = mixed_inverse * (keep[6] - mixed_plain * second)

    source = (col % 2) * 2 + core
    slot = low * 64 + (col // 2) * 8 + part

    def grad_copy(q):
        return remote(s3.at[q], r3.at[slot], 4, ((q % 8) * 4 + source, q // 8))

    def send_grad(k, carry):
        grad_copy((mine + k) % 128).start()
        return carry

    lax.fori_loop(1, 128, send_grad, 0)

    @pl.when(same)
    def _():
        pltpu.make_async_copy(s3.at[mine], r3.at[slot], recv_sem.at[4]).start()

    @pl.when(jnp.logical_not(same))
    def _():
        grad_copy(mine).start()

    out_value = product(split(out_proj.T), split(mixed_plain * mg))
    keep[6] = product(split(out_gate_ref[...]), split(keep[5] * out_value))

    wait(r3, recv_sem.at[4])
    for half in range(2):
        for n in range(12):
            grad_x[half, 8 * n:8 * n + 8, :] = jnp.concatenate(
                [r3[64 * half + 8 * b:64 * half + 8 * b + 8, 0, 24 * n:24 * n + 24] for b in range(8)], axis=1)
    right = right_all()
    dl_out[...] = product(split(grad_x[1 - low]), right)
    send_dl = remote(dl_out, dl_in, 5, x_peer)
    send_dl.start()
    grad_t = grad_x[...].reshape(192, 192).T
    dr = product(split(grad_t), split(left_x[...].reshape(192, 384)))
    for t in range(3):
        dr_full[t] = dr[:, 128 * t:128 * t + 128]
    for side in range(2):
        for n in range(12):
            for t in range(3):
                dr_t[side, 8 * n:8 * n + 8, 128 * t:128 * t + 128] = dr_full[
                    t, pl.ds(12 * side + n, 8, stride=24), :]
    send_dr = remote(dr_t.at[1 - core], dr_in, 6, core_peer)
    send_dr.start()
    dl_own[...] = product(split(grad_x[low]), right)
    send_dr.wait_recv()
    send_dl.wait_recv()
    dl = dl_own[...] + dl_in[...]
    dr = dr_t[core] + dr_in[...]
    for c in range(16):
        s4[8 * c:8 * c + 8, 0, :] = jnp.concatenate(
            [x[8 * n:8 * n + 8, 24 * c:24 * c + 24] for x in (dl, dr) for n in range(12)], axis=1)

    def send_back(k, carry):
        q = (mine + k) % 128
        remote(s4.at[q], r4.at[mine], 7, ((q % 8) * 4 + quarter, q // 8)).start()
        return carry

    lax.fori_loop(1, 128, send_back, 0)
    pltpu.make_async_copy(s4.at[mine], r4.at[mine], recv_sem.at[7]).start()

    wait(r4, recv_sem.at[7])
    dl = r4[:, 0, 0:288]
    dr = r4[:, 0, 288:576]
    stacked = jnp.concatenate([dl * keep[2], dl * keep[1], dr * keep[4], dr * keep[3]], axis=0)
    weights = jnp.concatenate([gate_a_ref[...], proj_a_ref[...], gate_b_ref[...], proj_b_ref[...]], axis=1)
    grad = (product(split(weights), split(stacked)) + keep[6]) * ng
    plain = keep[0]
    grad = stats[0:1] * (grad - mean0(grad) - plain * mean0(grad * plain))
    out_ref[...] = grad.T.reshape(12, 24, 128)

    send_left.wait_send()
    send_right.wait_send()
    send_dl.wait_send()
    send_dr.wait_send()
    wait(s1.at[pl.ds(0, 127)], send_sem.at[0])
    wait(s4.at[pl.ds(0, 127)], send_sem.at[7])
    wait(s2.at[pl.ds(0, 127)], send_sem.at[3])
    wait(s3.at[pl.ds(0, 127)], send_sem.at[4])

    @pl.when(jnp.logical_not(same))
    def _():
        wait(s2.at[0], send_sem.at[3])
        wait(s3.at[0], send_sem.at[4])


def local(pair, cotangent, norm_gain, gate_a, proj_a, gate_b, proj_b, mix_gain, out_gate, out_proj):
    def vmem(*shape):
        return pltpu.VMEM(shape, F32)

    return pl.pallas_call(
        kernel,
        out_shape=jax.ShapeDtypeStruct(pair.shape, F32),
        in_specs=[pl.BlockSpec(memory_space=pltpu.VMEM)] * 10,
        out_specs=pl.BlockSpec(memory_space=pltpu.VMEM),
        scratch_shapes=[
            vmem(128, 1, 576), vmem(128, 1, 576),
            vmem(2, 96, 384), vmem(2, 96, 384), vmem(3, 192, 128),
            vmem(128, 1, 288), vmem(128, 1, 288),
            vmem(128, 1, 288), vmem(128, 1, 288),
            vmem(2, 96, 192),
            vmem(96, 384), vmem(96, 384), vmem(96, 384),
            vmem(3, 192, 128), vmem(2, 96, 384), vmem(96, 384),
            vmem(128, 1, 576), vmem(128, 1, 576),
            vmem(8, 128, 288), vmem(8, 288),
            pltpu.SemaphoreType.DMA((8,)), pltpu.SemaphoreType.DMA((8,)), pltpu.SemaphoreType.REGULAR,
        ],
        compiler_params=pltpu.CompilerParams(
            collective_id=0, has_side_effects=True, vmem_limit_bytes=48 * 1024 * 1024),
    )(pair, cotangent, norm_gain.reshape(1, 128), gate_a, proj_a, gate_b, proj_b, mix_gain.reshape(1, 128),
      out_gate, out_proj)


def solution(mesh):
    placed = (P("row", "col", None), P("row", "col", None), P(), P(), P(), P(), P(), P(), P(), P())
    return jax.shard_map(
        local, mesh=mesh, in_specs=placed, out_specs=P("row", "col", None), check_vma=False)
```

```python
import jax
import jax.numpy as jnp
from jax import lax
from jax.experimental import pallas as pl
from jax.experimental.pallas import tpu as pltpu
from jax.sharding import PartitionSpec as P

MESH = pl.DeviceIdType.MESH
F32 = jnp.float32
NN = (((1,), (0,)), ((), ()))
NT = (((1,), (1,)), ((), ()))


def split(values):
    high = values.astype(jnp.bfloat16)
    return high, (values - high.astype(F32)).astype(jnp.bfloat16)


def product(a, b, dims=NN):
    def one(x, y):
        return lax.dot_general(x, y, dims, preferred_element_type=F32)

    return one(a[0], b[1]) + one(a[1], b[0]) + one(a[0], b[0])


def column(row):
    return jnp.broadcast_to(row, (8, 128)).T[:, 0:1]


def mean0(values):
    return jnp.mean(values, axis=0, keepdims=True)


def kernel(pair_hbm, cot_hbm, norm_gain_hbm, gate_a_hbm, proj_a_hbm, gate_b_hbm, proj_b_hbm, mix_gain_hbm,
           out_gate_hbm, out_proj_hbm, out_ref,
           pair_ref, cot_ref, gains, weights_ref, out_proj_ref, s1, r1, left_x, right_t, right_x, s2, r2, s3, r3, grad_x, dl_out, dl_in, dl_own, dr_full, dr_t, dr_in,
           s4, r4, keep, stats, load_sem, send_sem, recv_sem):
    row = lax.axis_index("row")
    col = lax.axis_index("col")
    core = lax.rem(row, 2)
    low = lax.rem(lax.div(row, 2), 2)
    part = lax.div(row, 4)
    quarter = lax.rem(row, 4)
    mine = col * 8 + part
    x_peer = (row + 2 - 4 * low, col)
    core_peer = (row + 1 - 2 * core, col)

    loads = [
        pltpu.make_async_copy(source, target, load_sem.at[i])
        for i, (source, target) in enumerate([
            (pair_hbm, pair_ref),
            (norm_gain_hbm, gains.at[0]),
            (gate_a_hbm, weights_ref.at[:, pl.ds(0, 128)]),
            (proj_a_hbm, weights_ref.at[:, pl.ds(128, 128)]),
            (gate_b_hbm, weights_ref.at[:, pl.ds(256, 128)]),
            (proj_b_hbm, weights_ref.at[:, pl.ds(384, 128)]),
            (out_gate_hbm, weights_ref.at[:, pl.ds(512, 128)]),
            (mix_gain_hbm, gains.at[1]),
            (cot_hbm, cot_ref),
            (out_proj_hbm, out_proj_ref),
        ])
    ]
    for load in loads:
        load.start()

    barrier = pltpu.get_barrier_semaphore()

    def greet(device):
        pl.semaphore_signal(barrier, inc=1, device_id=device, device_id_type=MESH)

    def mod(value, size):
        return lax.rem(value, size)

    y_here, z_here = lax.div(col, 2), lax.div(row, 8) * 2 + lax.rem(col, 2)
    z_all = [mod(z_here + t, 8) for t in range(8)]
    z_place = [lax.div(z, 2) * 2 for z in z_all]
    z_column = [lax.rem(z, 2) for z in z_all]
    x_place = [lax.rem(part + t, 2) for t in range(2)]

    def y_far(step):
        return mod(y_here + 4 + lax.div(step + 1, 2) * (1 - 2 * mod(step, 2)), 8) * 2

    inner = sorted(((z, x) for z in range(8) for x in range(2)), key=lambda o: -min(o[0], 8 - o[0]) - 2 * o[1])

    def each_channel(visit):
        def one(step, carry):
            column = y_far(step)
            for z, x in inner:
                visit(z_place[z] + x_place[x], column + z_column[z])
            return carry

        lax.fori_loop(0, 7, one, 0)
        for z, x in inner[:-1]:
            visit(z_place[z] + x_place[x], y_here * 2 + z_column[z])

    greet(x_peer)
    greet(core_peer)
    each_channel(lambda place, column: greet((place * 4 + quarter, column)))

    def remote(src, dst, phase, device):
        return pltpu.make_async_remote_copy(
            src_ref=src, dst_ref=dst, send_sem=send_sem.at[phase], recv_sem=recv_sem.at[phase],
            device_id=device, device_id_type=MESH)

    def wait(ref, sem):
        pltpu.make_async_copy(ref, ref, sem).wait()

    for load in loads[0:2]:
        load.wait()
    ng = column(gains[0])
    pair = pair_ref[...].reshape(288, 128).T
    centred = pair - mean0(pair)
    inverse = lax.rsqrt(mean0(centred * centred) + 1e-05)
    plain = centred * inverse
    normed = split(plain * ng)
    for load in loads[2:7]:
        load.wait()
    projected = product(split(weights_ref[...].T), normed)
    left_gate = jax.nn.sigmoid(projected[0:128])
    left_value = projected[128:256]
    right_gate = jax.nn.sigmoid(projected[256:384])
    right_value = projected[384:512]
    s1[:, 0, :] = jnp.concatenate([left_gate * left_value, right_gate * right_value], axis=1)

    pl.semaphore_wait(barrier, 129)

    def send_edges(place, column):
        remote(s1.at[column * 8 + place], r1.at[mine], 0, (place * 4 + quarter, column)).start()

    each_channel(send_edges)
    pltpu.make_async_copy(s1.at[mine], r1.at[mine], recv_sem.at[0]).start()

    keep[0] = plain
    keep[1] = left_gate
    keep[2] = left_value * left_gate * (1.0 - left_gate)
    keep[3] = right_gate
    keep[4] = right_value * right_gate * (1.0 - right_gate)
    for load in loads[7:10]:
        load.wait()
    mg = column(gains[1])
    out_sig = jax.nn.sigmoid(projected[512:640])
    grad_value = cot_ref[...].reshape(288, 128).T * out_sig
    keep[5] = grad_value * (1.0 - out_sig)
    out_proj = out_proj_ref[...]
    scaled = product(split(out_proj), split(grad_value)) * mg
    keep[6] = scaled - mean0(scaled)
    keep[7] = scaled
    stats[0:1] = inverse

    wait(r1, recv_sem.at[0])
    for n in range(12):
        left_x[low, 8 * n:8 * n + 8, :] = jnp.concatenate(
            [r1[8 * c:8 * c + 8, 0, 24 * n:24 * n + 24] for c in range(16)], axis=1)
    send_left = remote(left_x.at[low], left_x.at[low], 1, x_peer)
    send_left.start()
    for n in range(12):
        right_t[core, 8 * n:8 * n + 8, :] = jnp.concatenate(
            [r1[8 * c:8 * c + 8, 0, 24 * n + 288:24 * n + 312] for c in range(16)], axis=1)
    send_right = remote(right_t.at[core], right_t.at[core], 2, core_peer)
    send_right.start()
    send_right.wait_recv()
    for side in range(2):
        for n in range(12):
            for t in range(3):
                right_x[t, pl.ds(12 * side + n, 8, stride=24), :] = right_t[
                    side, 8 * n:8 * n + 8, 128 * t:128 * t + 128]

    def right_all():
        return split(jnp.concatenate([right_x[t] for t in range(3)], axis=1))

    right = right_all()

    same = lax.rem(col, 2) == low
    slot = low * 64 + y_here * 8 + part

    def mix(half):
        mixed = product(split(left_x[half]), right, NT)
        for b in range(8):
            s2[pl.ds(half * 64 + 8 * b, 8), 0, :] = jnp.concatenate(
                [mixed[8 * n:8 * n + 8, 24 * b:24 * b + 24] for n in range(12)], axis=1)

    def mixed_copy(half, column, place):
        return remote(s2.at[half * 64 + lax.div(column, 2) * 8 + place], r2.at[mine], 3,
                      (place * 4 + half * 2 + core, column + low))

    z_half = [lax.rem(lax.div(row, 8) + t, 4) * 2 for t in range(4)]
    inner_half = ((2, 1), (2, 0), (1, 1), (3, 1), (1, 0), (3, 0), (0, 1), (0, 0))

    def send_mixed(half, last):
        def one(step, carry):
            column = y_far(step)
            for z, x in inner_half:
                mixed_copy(half, column, z_half[z] + x_place[x]).start()
            return carry

        lax.fori_loop(0, 7, one, 0)
        for z, x in inner_half[:last]:
            mixed_copy(half, y_here * 2, z_half[z] + x_place[x]).start()

    mix(low)

    send_mixed(low, 7)

    @pl.when(same)
    def _():
        pltpu.make_async_copy(s2.at[slot], r2.at[mine], recv_sem.at[3]).start()

    @pl.when(jnp.logical_not(same))
    def _():
        mixed_copy(low, y_here * 2, part).start()

    send_left.wait_recv()
    mix(1 - low)

    send_mixed(1 - low, 8)

    wait(r2, recv_sem.at[3])
    mixed = r2[:, 0, :]
    mixed = mixed - mean0(mixed)
    mixed_inverse = lax.rsqrt(mean0(mixed * mixed) + 1e-05)
    mixed_plain = mixed * mixed_inverse
    second = mean0(keep[7] * mixed_plain)
    s3[:, 0, :] = mixed_inverse * (keep[6] - mixed_plain * second)

    source = lax.rem(col, 2) * 2 + core

    def grad_copy(place, column):
        return remote(s3.at[column * 8 + place], r3.at[slot], 4, (place * 4 + source, column))

    each_channel(lambda place, column: grad_copy(place, column).start())

    @pl.when(same)
    def _():
        pltpu.make_async_copy(s3.at[mine], r3.at[slot], recv_sem.at[4]).start()

    @pl.when(jnp.logical_not(same))
    def _():
        grad_copy(part, col).start()

    out_value = product(split(out_proj.T), split(mixed_plain * mg))
    keep[6] = product(split(weights_ref[:, 512:640]), split(keep[5] * out_value))

    wait(r3, recv_sem.at[4])
    for half in range(2):
        for n in range(12):
            grad_x[half, 8 * n:8 * n + 8, :] = jnp.concatenate(
                [r3[64 * half + 8 * b:64 * half + 8 * b + 8, 0, 24 * n:24 * n + 24] for b in range(8)], axis=1)
    right = right_all()
    dl_out[...] = product(split(grad_x[1 - low]), right)
    send_dl = remote(dl_out, dl_in, 5, x_peer)
    send_dl.start()
    grad_t = grad_x[...].reshape(192, 192).T
    dr = product(split(grad_t), split(left_x[...].reshape(192, 384)))
    for t in range(3):
        dr_full[t] = dr[:, 128 * t:128 * t + 128]
    for side in range(2):
        for n in range(12):
            for t in range(3):
                dr_t[side, 8 * n:8 * n + 8, 128 * t:128 * t + 128] = dr_full[
                    t, pl.ds(12 * side + n, 8, stride=24), :]
    send_dr = remote(dr_t.at[1 - core], dr_in, 6, core_peer)
    send_dr.start()
    dl_own[...] = product(split(grad_x[low]), right)
    send_dr.wait_recv()
    send_dl.wait_recv()
    dl = dl_own[...] + dl_in[...]
    dr = dr_t[core] + dr_in[...]
    for c in range(16):
        s4[8 * c:8 * c + 8, 0, :] = jnp.concatenate(
            [x[8 * n:8 * n + 8, 24 * c:24 * c + 24] for x in (dl, dr) for n in range(12)], axis=1)

    def send_back(place, column):
        remote(s4.at[column * 8 + place], r4.at[mine], 7, (place * 4 + quarter, column)).start()

    each_channel(send_back)
    pltpu.make_async_copy(s4.at[mine], r4.at[mine], recv_sem.at[7]).start()

    wait(r4, recv_sem.at[7])
    dl = r4[:, 0, 0:288]
    dr = r4[:, 0, 288:576]
    stacked = jnp.concatenate([dl * keep[2], dl * keep[1], dr * keep[4], dr * keep[3]], axis=0)
    grad = (product(split(weights_ref[:, 0:512]), split(stacked)) + keep[6]) * ng
    plain = keep[0]
    grad = stats[0:1] * (grad - mean0(grad) - plain * mean0(grad * plain))
    out_ref[...] = grad.T.reshape(12, 24, 128)

    send_left.wait_send()
    send_right.wait_send()
    send_dl.wait_send()
    send_dr.wait_send()
    wait(s1.at[pl.ds(0, 127)], send_sem.at[0])
    wait(s4.at[pl.ds(0, 127)], send_sem.at[7])
    wait(s2.at[pl.ds(0, 127)], send_sem.at[3])
    wait(s3.at[pl.ds(0, 127)], send_sem.at[4])

    @pl.when(jnp.logical_not(same))
    def _():
        wait(s2.at[0], send_sem.at[3])
        wait(s3.at[0], send_sem.at[4])


def local(pair, cotangent, norm_gain, gate_a, proj_a, gate_b, proj_b, mix_gain, out_gate, out_proj):
    def vmem(*shape):
        return pltpu.VMEM(shape, F32)

    return pl.pallas_call(
        kernel,
        out_shape=jax.ShapeDtypeStruct(pair.shape, F32),
        in_specs=[pl.BlockSpec(memory_space=pltpu.HBM)] * 10,
        out_specs=pl.BlockSpec(memory_space=pltpu.VMEM),
        scratch_shapes=[
            vmem(12, 24, 128), vmem(12, 24, 128), vmem(2, 1, 128), vmem(128, 640), vmem(128, 128),
            vmem(128, 1, 576), vmem(128, 1, 576),
            vmem(2, 96, 384), vmem(2, 96, 384), vmem(3, 192, 128),
            vmem(128, 1, 288), vmem(128, 1, 288),
            vmem(128, 1, 288), vmem(128, 1, 288),
            vmem(2, 96, 192),
            vmem(96, 384), vmem(96, 384), vmem(96, 384),
            vmem(3, 192, 128), vmem(2, 96, 384), vmem(96, 384),
            vmem(128, 1, 576), vmem(128, 1, 576),
            vmem(8, 128, 288), vmem(8, 288),
            pltpu.SemaphoreType.DMA((10,)), pltpu.SemaphoreType.DMA((8,)), pltpu.SemaphoreType.DMA((8,)),
        ],
        compiler_params=pltpu.CompilerParams(
            collective_id=0, has_side_effects=True, vmem_limit_bytes=64 * 1024 * 1024 - 65536),
    )(pair, cotangent, norm_gain.reshape(1, 128), gate_a, proj_a, gate_b, proj_b, mix_gain.reshape(1, 128),
      out_gate, out_proj)


def solution(mesh):
    placed = (P("row", "col", None), P("row", "col", None), P(), P(), P(), P(), P(), P(), P(), P())
    return jax.shard_map(
        local, mesh=mesh, in_specs=placed, out_specs=P("row", "col", None), check_vma=False)
```

```python
import jax
import jax.numpy as jnp
from jax import lax
from jax.experimental import pallas as pl
from jax.experimental.pallas import tpu as pltpu
from jax.sharding import PartitionSpec as P


def far_first(sizes, hops):
    steps = [(y, z, x) for y in range(sizes[0]) for z in range(sizes[1]) for x in range(sizes[2])]
    return sorted(steps, key=lambda s: (-hops(*s), (s[0] * 41 + s[1] * 23 + s[2] * 67 + s[0] * s[1] * 29) * 53 % 131))


def ring(step):
    return min(step, 8 - step)


CHANNELS = far_first((8, 8, 2), lambda y, z, x: ring(y) + ring(z) + 2 * x)[:-1]
SAME_X = far_first((8, 4, 2), lambda y, z, x: ring(y) + ring(2 * z) + 2 * x)[:-1]
OTHER_X = far_first((8, 4, 2), lambda y, z, x: ring(y) + ring(2 * z))
VMEM = 64 * 1024 * 1024 - 65536
MESH = pl.DeviceIdType.MESH
F32 = jnp.float32
NN = (((1,), (0,)), ((), ()))
NT = (((1,), (1,)), ((), ()))


def split(values):
    high = values.astype(jnp.bfloat16)
    return high, (values - high.astype(F32)).astype(jnp.bfloat16)


def product(a, b, dims=NN):
    def one(x, y):
        return lax.dot_general(x, y, dims, preferred_element_type=F32)

    return one(a[0], b[1]) + one(a[1], b[0]) + one(a[0], b[0])


def column(row):
    return jnp.broadcast_to(row, (8, 128)).T[:, 0:1]


def mean0(values):
    return jnp.mean(values, axis=0, keepdims=True)


def kernel(pair_hbm, cot_hbm, norm_gain_hbm, gate_a_hbm, proj_a_hbm, gate_b_hbm, proj_b_hbm, mix_gain_hbm,
           out_gate_hbm, out_proj_hbm, out_ref,
           pair_ref, cot_ref, gains, weights_ref, out_proj_ref, s1, r1, left_x, right_t, right_x, s2, r2, s3, r3, grad_x, dl_out, dl_in, dl_own, dr_full, dr_t, dr_in,
           s4, r4, keep, stats, load_sem, send_sem, recv_sem):
    row = lax.axis_index("row")
    col = lax.axis_index("col")
    core = lax.rem(row, 2)
    low = lax.rem(lax.div(row, 2), 2)
    part = lax.div(row, 4)
    quarter = lax.rem(row, 4)
    mine = col * 8 + part
    x_peer = (row + 2 - 4 * low, col)
    core_peer = (row + 1 - 2 * core, col)

    loads = [
        pltpu.make_async_copy(source, target, load_sem.at[i])
        for i, (source, target) in enumerate([
            (pair_hbm, pair_ref),
            (norm_gain_hbm, gains.at[0]),
            (gate_a_hbm, weights_ref.at[:, pl.ds(0, 128)]),
            (proj_a_hbm, weights_ref.at[:, pl.ds(128, 128)]),
            (gate_b_hbm, weights_ref.at[:, pl.ds(256, 128)]),
            (proj_b_hbm, weights_ref.at[:, pl.ds(384, 128)]),
            (out_gate_hbm, weights_ref.at[:, pl.ds(512, 128)]),
            (mix_gain_hbm, gains.at[1]),
            (cot_hbm, cot_ref),
            (out_proj_hbm, out_proj_ref),
        ])
    ]
    for load in loads:
        load.start()

    barrier = pltpu.get_barrier_semaphore()

    def greet(device):
        pl.semaphore_signal(barrier, inc=1, device_id=device, device_id_type=MESH)

    y_here, z_here = lax.div(col, 2), lax.div(row, 8) * 2 + lax.rem(col, 2)
    y_column = [lax.rem(y_here + t, 8) * 2 for t in range(8)]
    z_all = [lax.rem(z_here + t, 8) for t in range(8)]
    z_place = [lax.div(z, 2) * 2 for z in z_all]
    z_column = [lax.rem(z, 2) for z in z_all]
    x_place = [lax.rem(part + t, 2) for t in range(2)]

    def each_channel(visit):
        for y, z, x in CHANNELS:
            visit(z_place[z] + x_place[x], y_column[y] + z_column[z])

    greet(x_peer)
    greet(core_peer)
    each_channel(lambda place, column: greet((place * 4 + quarter, column)))

    def remote(src, dst, phase, device):
        return pltpu.make_async_remote_copy(
            src_ref=src, dst_ref=dst, send_sem=send_sem.at[phase], recv_sem=recv_sem.at[phase],
            device_id=device, device_id_type=MESH)

    def wait(ref, sem):
        pltpu.make_async_copy(ref, ref, sem).wait()

    for load in loads[0:2]:
        load.wait()
    ng = column(gains[0])
    pair = pair_ref[...].reshape(288, 128).T
    centred = pair - mean0(pair)
    inverse = lax.rsqrt(mean0(centred * centred) + 1e-05)
    plain = centred * inverse
    normed = split(plain * ng)
    for load in loads[2:7]:
        load.wait()
    projected = product(split(weights_ref[...].T), normed)
    left_gate = jax.nn.sigmoid(projected[0:128])
    left_value = projected[128:256]
    right_gate = jax.nn.sigmoid(projected[256:384])
    right_value = projected[384:512]
    s1[:, 0, :] = jnp.concatenate([left_gate * left_value, right_gate * right_value], axis=1)

    pl.semaphore_wait(barrier, 129)

    def send_edges(place, column):
        remote(s1.at[column * 8 + place], r1.at[mine], 0, (place * 4 + quarter, column)).start()

    each_channel(send_edges)
    pltpu.make_async_copy(s1.at[mine], r1.at[mine], recv_sem.at[0]).start()

    keep[0] = plain
    keep[1] = left_gate
    keep[2] = left_value * left_gate * (1.0 - left_gate)
    keep[3] = right_gate
    keep[4] = right_value * right_gate * (1.0 - right_gate)
    for load in loads[7:10]:
        load.wait()
    mg = column(gains[1])
    out_sig = jax.nn.sigmoid(projected[512:640])
    grad_value = cot_ref[...].reshape(288, 128).T * out_sig
    keep[5] = grad_value * (1.0 - out_sig)
    out_proj = out_proj_ref[...]
    scaled = product(split(out_proj), split(grad_value)) * mg
    keep[6] = scaled - mean0(scaled)
    keep[7] = scaled
    stats[0:1] = inverse

    wait(r1, recv_sem.at[0])
    for n in range(12):
        left_x[low, 8 * n:8 * n + 8, :] = jnp.concatenate(
            [r1[8 * c:8 * c + 8, 0, 24 * n:24 * n + 24] for c in range(16)], axis=1)
    send_left = remote(left_x.at[low], left_x.at[low], 1, x_peer)
    send_left.start()
    for n in range(12):
        right_t[core, 8 * n:8 * n + 8, :] = jnp.concatenate(
            [r1[8 * c:8 * c + 8, 0, 24 * n + 288:24 * n + 312] for c in range(16)], axis=1)
    send_right = remote(right_t.at[core], right_t.at[core], 2, core_peer)
    send_right.start()
    send_right.wait_recv()
    for side in range(2):
        for n in range(12):
            for t in range(3):
                right_x[t, pl.ds(12 * side + n, 8, stride=24), :] = right_t[
                    side, 8 * n:8 * n + 8, 128 * t:128 * t + 128]

    def right_all():
        return split(jnp.concatenate([right_x[t] for t in range(3)], axis=1))

    right = right_all()

    same = lax.rem(col, 2) == low
    slot = low * 64 + y_here * 8 + part

    def mix(half):
        mixed = product(split(left_x[half]), right, NT)
        for b in range(8):
            s2[pl.ds(half * 64 + 8 * b, 8), 0, :] = jnp.concatenate(
                [mixed[8 * n:8 * n + 8, 24 * b:24 * b + 24] for n in range(12)], axis=1)

    def mixed_copy(half, column, place):
        return remote(s2.at[half * 64 + lax.div(column, 2) * 8 + place], r2.at[mine], 3,
                      (place * 4 + half * 2 + core, column + low))

    z_half = [lax.rem(lax.div(row, 8) + t, 4) * 2 for t in range(4)]
    def send_mixed(half, steps):
        for y, z, x in steps:
            mixed_copy(half, y_column[y], z_half[z] + x_place[x]).start()

    mix(low)

    send_mixed(low, SAME_X)

    @pl.when(same)
    def _():
        pltpu.make_async_copy(s2.at[slot], r2.at[mine], recv_sem.at[3]).start()

    @pl.when(jnp.logical_not(same))
    def _():
        mixed_copy(low, y_column[0], part).start()

    send_left.wait_recv()
    mix(1 - low)

    send_mixed(1 - low, OTHER_X)

    wait(r2, recv_sem.at[3])
    mixed = r2[:, 0, :]
    mixed = mixed - mean0(mixed)
    mixed_inverse = lax.rsqrt(mean0(mixed * mixed) + 1e-05)
    mixed_plain = mixed * mixed_inverse
    second = mean0(keep[7] * mixed_plain)
    s3[:, 0, :] = mixed_inverse * (keep[6] - mixed_plain * second)

    source = lax.rem(col, 2) * 2 + core

    def grad_copy(place, column):
        return remote(s3.at[column * 8 + place], r3.at[slot], 4, (place * 4 + source, column))

    each_channel(lambda place, column: grad_copy(place, column).start())

    @pl.when(same)
    def _():
        pltpu.make_async_copy(s3.at[mine], r3.at[slot], recv_sem.at[4]).start()

    @pl.when(jnp.logical_not(same))
    def _():
        grad_copy(part, col).start()

    out_value = product(split(out_proj.T), split(mixed_plain * mg))
    keep[6] = product(split(weights_ref[:, 512:640]), split(keep[5] * out_value))

    wait(r3, recv_sem.at[4])
    for half in range(2):
        for n in range(12):
            grad_x[half, 8 * n:8 * n + 8, :] = jnp.concatenate(
                [r3[64 * half + 8 * b:64 * half + 8 * b + 8, 0, 24 * n:24 * n + 24] for b in range(8)], axis=1)
    right = right_all()
    dl_out[...] = product(split(grad_x[1 - low]), right)
    send_dl = remote(dl_out, dl_in, 5, x_peer)
    send_dl.start()
    grad_t = grad_x[...].reshape(192, 192).T
    dr = product(split(grad_t), split(left_x[...].reshape(192, 384)))
    for t in range(3):
        dr_full[t] = dr[:, 128 * t:128 * t + 128]
    for side in range(2):
        for n in range(12):
            for t in range(3):
                dr_t[side, 8 * n:8 * n + 8, 128 * t:128 * t + 128] = dr_full[
                    t, pl.ds(12 * side + n, 8, stride=24), :]
    send_dr = remote(dr_t.at[1 - core], dr_in, 6, core_peer)
    send_dr.start()
    dl_own[...] = product(split(grad_x[low]), right)
    send_dr.wait_recv()
    send_dl.wait_recv()
    dl = dl_own[...] + dl_in[...]
    dr = dr_t[core] + dr_in[...]
    for c in range(16):
        s4[8 * c:8 * c + 8, 0, :] = jnp.concatenate(
            [x[8 * n:8 * n + 8, 24 * c:24 * c + 24] for x in (dl, dr) for n in range(12)], axis=1)

    def send_back(place, column):
        remote(s4.at[column * 8 + place], r4.at[mine], 7, (place * 4 + quarter, column)).start()

    each_channel(send_back)
    pltpu.make_async_copy(s4.at[mine], r4.at[mine], recv_sem.at[7]).start()

    wait(r4, recv_sem.at[7])
    dl = r4[:, 0, 0:288]
    dr = r4[:, 0, 288:576]
    stacked = jnp.concatenate([dl * keep[2], dl * keep[1], dr * keep[4], dr * keep[3]], axis=0)
    grad = (product(split(weights_ref[:, 0:512]), split(stacked)) + keep[6]) * ng
    plain = keep[0]
    grad = stats[0:1] * (grad - mean0(grad) - plain * mean0(grad * plain))
    out_ref[...] = grad.T.reshape(12, 24, 128)

    send_left.wait_send()
    send_right.wait_send()
    send_dl.wait_send()
    send_dr.wait_send()
    wait(s1.at[pl.ds(0, 127)], send_sem.at[0])
    wait(s4.at[pl.ds(0, 127)], send_sem.at[7])
    wait(s2.at[pl.ds(0, 127)], send_sem.at[3])
    wait(s3.at[pl.ds(0, 127)], send_sem.at[4])

    @pl.when(jnp.logical_not(same))
    def _():
        wait(s2.at[0], send_sem.at[3])
        wait(s3.at[0], send_sem.at[4])


def local(pair, cotangent, norm_gain, gate_a, proj_a, gate_b, proj_b, mix_gain, out_gate, out_proj):
    def vmem(*shape):
        return pltpu.VMEM(shape, F32)

    return pl.pallas_call(
        kernel,
        out_shape=jax.ShapeDtypeStruct(pair.shape, F32),
        in_specs=[pl.BlockSpec(memory_space=pltpu.HBM)] * 10,
        out_specs=pl.BlockSpec(memory_space=pltpu.VMEM),
        scratch_shapes=[
            vmem(12, 24, 128), vmem(12, 24, 128), vmem(2, 1, 128), vmem(128, 640), vmem(128, 128),
            vmem(128, 1, 576), vmem(128, 1, 576),
            vmem(2, 96, 384), vmem(2, 96, 384), vmem(3, 192, 128),
            vmem(128, 1, 288), vmem(128, 1, 288),
            vmem(128, 1, 288), vmem(128, 1, 288),
            vmem(2, 96, 192),
            vmem(96, 384), vmem(96, 384), vmem(96, 384),
            vmem(3, 192, 128), vmem(2, 96, 384), vmem(96, 384),
            vmem(128, 1, 576), vmem(128, 1, 576),
            vmem(8, 128, 288), vmem(8, 288),
            pltpu.SemaphoreType.DMA((10,)), pltpu.SemaphoreType.DMA((8,)), pltpu.SemaphoreType.DMA((8,)),
        ],
        compiler_params=pltpu.CompilerParams(
            collective_id=0, has_side_effects=True, vmem_limit_bytes=VMEM),
    )(pair, cotangent, norm_gain.reshape(1, 128), gate_a, proj_a, gate_b, proj_b, mix_gain.reshape(1, 128),
      out_gate, out_proj)


def solution(mesh):
    placed = (P("row", "col", None), P("row", "col", None), P(), P(), P(), P(), P(), P(), P(), P())
    return jax.shard_map(
        local, mesh=mesh, in_specs=placed, out_specs=P("row", "col", None), check_vma=False)
```

```python
import random

import jax
import jax.numpy as jnp
from jax import lax
from jax.experimental import pallas as pl
from jax.experimental.pallas import tpu as pltpu
from jax.sharding import PartitionSpec as P


def far_first(sizes, hops):
    steps = [(y, z, x) for y in range(sizes[0]) for z in range(sizes[1]) for x in range(sizes[2])]
    random.Random(0).shuffle(steps)
    return sorted(steps, key=lambda s: -hops(*s))


def ring(step):
    return min(step, 8 - step)


CHANNELS = far_first((8, 8, 2), lambda y, z, x: ring(y) + ring(z) + 2 * x)[:-1]
SAME_X = far_first((8, 4, 2), lambda y, z, x: ring(y) + ring(2 * z) + 2 * x)[:-1]
OTHER_X = far_first((8, 4, 2), lambda y, z, x: ring(y) + ring(2 * z))
VMEM = 64 * 1024 * 1024 - 65536
MESH = pl.DeviceIdType.MESH
F32 = jnp.float32
NN = (((1,), (0,)), ((), ()))
NT = (((1,), (1,)), ((), ()))


def split(values):
    high = values.astype(jnp.bfloat16)
    return high, (values - high.astype(F32)).astype(jnp.bfloat16)


def product(a, b, dims=NN):
    def one(x, y):
        return lax.dot_general(x, y, dims, preferred_element_type=F32)

    return one(a[0], b[1]) + one(a[1], b[0]) + one(a[0], b[0])


def column(row):
    return jnp.broadcast_to(row, (8, 128)).T[:, 0:1]


def mean0(values):
    return jnp.mean(values, axis=0, keepdims=True)


def kernel(pair_hbm, cot_hbm, norm_gain_hbm, gate_a_hbm, proj_a_hbm, gate_b_hbm, proj_b_hbm, mix_gain_hbm,
           out_gate_hbm, out_proj_hbm, out_ref,
           pair_ref, cot_ref, gains, weights_ref, out_proj_ref, s1, r1, left_x, right_t, right_x, s2, r2, s3, r3, grad_x, dl_out, dl_in, dl_own, dr_full, dr_t, dr_in,
           s4, r4, keep, stats, load_sem, send_sem, recv_sem):
    row = lax.axis_index("row")
    col = lax.axis_index("col")
    core = lax.rem(row, 2)
    low = lax.rem(lax.div(row, 2), 2)
    part = lax.div(row, 4)
    quarter = lax.rem(row, 4)
    mine = col * 8 + part
    x_peer = (row + 2 - 4 * low, col)
    core_peer = (row + 1 - 2 * core, col)

    loads = [
        pltpu.make_async_copy(source, target, load_sem.at[i])
        for i, (source, target) in enumerate([
            (pair_hbm, pair_ref),
            (norm_gain_hbm, gains.at[0]),
            (gate_a_hbm, weights_ref.at[:, pl.ds(0, 128)]),
            (proj_a_hbm, weights_ref.at[:, pl.ds(128, 128)]),
            (gate_b_hbm, weights_ref.at[:, pl.ds(256, 128)]),
            (proj_b_hbm, weights_ref.at[:, pl.ds(384, 128)]),
            (out_gate_hbm, weights_ref.at[:, pl.ds(512, 128)]),
            (mix_gain_hbm, gains.at[1]),
            (cot_hbm, cot_ref),
            (out_proj_hbm, out_proj_ref),
        ])
    ]
    for load in loads:
        load.start()

    barrier = pltpu.get_barrier_semaphore()

    def greet(device):
        pl.semaphore_signal(barrier, inc=1, device_id=device, device_id_type=MESH)

    y_here, z_here = lax.div(col, 2), lax.div(row, 8) * 2 + lax.rem(col, 2)
    y_column = [lax.rem(y_here + t, 8) * 2 for t in range(8)]
    z_all = [lax.rem(z_here + t, 8) for t in range(8)]
    z_place = [lax.div(z, 2) * 2 for z in z_all]
    z_column = [lax.rem(z, 2) for z in z_all]
    x_place = [lax.rem(part + t, 2) for t in range(2)]

    def each_channel(visit):
        for y, z, x in CHANNELS:
            visit(z_place[z] + x_place[x], y_column[y] + z_column[z])

    greet(x_peer)
    greet(core_peer)
    each_channel(lambda place, column: greet((place * 4 + quarter, column)))

    def remote(src, dst, phase, device):
        return pltpu.make_async_remote_copy(
            src_ref=src, dst_ref=dst, send_sem=send_sem.at[phase], recv_sem=recv_sem.at[phase],
            device_id=device, device_id_type=MESH)

    def wait(ref, sem):
        pltpu.make_async_copy(ref, ref, sem).wait()

    for load in loads[0:2]:
        load.wait()
    ng = column(gains[0])
    pair = pair_ref[...].reshape(288, 128).T
    centred = pair - mean0(pair)
    inverse = lax.rsqrt(mean0(centred * centred) + 1e-05)
    plain = centred * inverse
    normed = split(plain * ng)
    for load in loads[2:7]:
        load.wait()
    projected = product(split(weights_ref[...].T), normed)
    left_gate = jax.nn.sigmoid(projected[0:128])
    left_value = projected[128:256]
    right_gate = jax.nn.sigmoid(projected[256:384])
    right_value = projected[384:512]
    s1[:, 0, :] = jnp.concatenate([left_gate * left_value, right_gate * right_value], axis=1)

    pl.semaphore_wait(barrier, 129)

    def send_edges(place, column):
        remote(s1.at[column * 8 + place], r1.at[mine], 0, (place * 4 + quarter, column)).start()

    each_channel(send_edges)
    pltpu.make_async_copy(s1.at[mine], r1.at[mine], recv_sem.at[0]).start()

    keep[0] = plain
    keep[1] = left_gate
    keep[2] = left_value * left_gate * (1.0 - left_gate)
    keep[3] = right_gate
    keep[4] = right_value * right_gate * (1.0 - right_gate)
    for load in loads[7:10]:
        load.wait()
    mg = column(gains[1])
    out_sig = jax.nn.sigmoid(projected[512:640])
    grad_value = cot_ref[...].reshape(288, 128).T * out_sig
    keep[5] = grad_value * (1.0 - out_sig)
    out_proj = out_proj_ref[...]
    scaled = product(split(out_proj), split(grad_value)) * mg
    keep[6] = scaled - mean0(scaled)
    keep[7] = scaled
    stats[0:1] = inverse

    wait(r1, recv_sem.at[0])
    for n in range(12):
        left_x[low, 8 * n:8 * n + 8, :] = jnp.concatenate(
            [r1[8 * c:8 * c + 8, 0, 24 * n:24 * n + 24] for c in range(16)], axis=1)
    send_left = remote(left_x.at[low], left_x.at[low], 1, x_peer)
    send_left.start()
    for n in range(12):
        right_t[core, 8 * n:8 * n + 8, :] = jnp.concatenate(
            [r1[8 * c:8 * c + 8, 0, 24 * n + 288:24 * n + 312] for c in range(16)], axis=1)
    send_right = remote(right_t.at[core], right_t.at[core], 2, core_peer)
    send_right.start()
    send_right.wait_recv()
    for side in range(2):
        for n in range(12):
            for t in range(3):
                right_x[t, pl.ds(12 * side + n, 8, stride=24), :] = right_t[
                    side, 8 * n:8 * n + 8, 128 * t:128 * t + 128]

    def right_all():
        return split(jnp.concatenate([right_x[t] for t in range(3)], axis=1))

    right = right_all()

    same = lax.rem(col, 2) == low
    slot = low * 64 + y_here * 8 + part

    def mix(half):
        mixed = product(split(left_x[half]), right, NT)
        for b in range(8):
            s2[pl.ds(half * 64 + 8 * b, 8), 0, :] = jnp.concatenate(
                [mixed[8 * n:8 * n + 8, 24 * b:24 * b + 24] for n in range(12)], axis=1)

    def mixed_copy(half, column, place):
        return remote(s2.at[half * 64 + lax.div(column, 2) * 8 + place], r2.at[mine], 3,
                      (place * 4 + half * 2 + core, column + low))

    z_half = [lax.rem(lax.div(row, 8) + t, 4) * 2 for t in range(4)]
    def send_mixed(half, steps):
        for y, z, x in steps:
            mixed_copy(half, y_column[y], z_half[z] + x_place[x]).start()

    mix(low)

    send_mixed(low, SAME_X)

    @pl.when(same)
    def _():
        pltpu.make_async_copy(s2.at[slot], r2.at[mine], recv_sem.at[3]).start()

    @pl.when(jnp.logical_not(same))
    def _():
        mixed_copy(low, y_column[0], part).start()

    send_left.wait_recv()
    mix(1 - low)

    send_mixed(1 - low, OTHER_X)

    wait(r2, recv_sem.at[3])
    mixed = r2[:, 0, :]
    mixed = mixed - mean0(mixed)
    mixed_inverse = lax.rsqrt(mean0(mixed * mixed) + 1e-05)
    mixed_plain = mixed * mixed_inverse
    second = mean0(keep[7] * mixed_plain)
    s3[:, 0, :] = mixed_inverse * (keep[6] - mixed_plain * second)

    source = lax.rem(col, 2) * 2 + core

    def grad_copy(place, column):
        return remote(s3.at[column * 8 + place], r3.at[slot], 4, (place * 4 + source, column))

    each_channel(lambda place, column: grad_copy(place, column).start())

    @pl.when(same)
    def _():
        pltpu.make_async_copy(s3.at[mine], r3.at[slot], recv_sem.at[4]).start()

    @pl.when(jnp.logical_not(same))
    def _():
        grad_copy(part, col).start()

    out_value = product(split(out_proj.T), split(mixed_plain * mg))
    keep[6] = product(split(weights_ref[:, 512:640]), split(keep[5] * out_value))

    right = right_all()
    left = split(left_x[...].reshape(192, 384))

    def turn_grad(half):
        for n in range(12):
            grad_x[half, 8 * n:8 * n + 8, :] = jnp.concatenate(
                [r3[pl.ds(64 * half + 8 * b, 8), 0, 24 * n:24 * n + 24] for b in range(8)], axis=1)

    wait(r3, recv_sem.at[4])
    turn_grad(1 - low)
    dl_out[...] = product(split(grad_x[1 - low]), right)
    send_dl = remote(dl_out, dl_in, 5, x_peer)
    send_dl.start()
    turn_grad(low)
    grad_t = grad_x[...].reshape(192, 192).T
    dr = product(split(grad_t), left)
    for t in range(3):
        dr_full[t] = dr[:, 128 * t:128 * t + 128]

    def turn_rows(side):
        for n in range(12):
            for t in range(3):
                dr_t[side, 8 * n:8 * n + 8, 128 * t:128 * t + 128] = dr_full[
                    t, pl.ds(12 * side + n, 8, stride=24), :]

    turn_rows(1 - core)
    send_dr = remote(dr_t.at[1 - core], dr_in, 6, core_peer)
    send_dr.start()
    turn_rows(core)
    dl_own[...] = product(split(grad_x[low]), right)
    send_dr.wait_recv()
    send_dl.wait_recv()
    dl = dl_own[...] + dl_in[...]
    dr = dr_t[core] + dr_in[...]
    for c in range(16):
        s4[8 * c:8 * c + 8, 0, :] = jnp.concatenate(
            [x[8 * n:8 * n + 8, 24 * c:24 * c + 24] for x in (dl, dr) for n in range(12)], axis=1)

    def send_back(place, column):
        remote(s4.at[column * 8 + place], r4.at[mine], 7, (place * 4 + quarter, column)).start()

    each_channel(send_back)
    pltpu.make_async_copy(s4.at[mine], r4.at[mine], recv_sem.at[7]).start()

    weights = split(weights_ref[:, 0:512])
    plain = keep[0]
    partial = keep[6]
    wait(r4, recv_sem.at[7])
    dl = r4[:, 0, 0:288]
    dr = r4[:, 0, 288:576]
    stacked = jnp.concatenate([dl * keep[2], dl * keep[1], dr * keep[4], dr * keep[3]], axis=0)
    grad = (product(weights, split(stacked)) + partial) * ng
    grad = stats[0:1] * (grad - mean0(grad) - plain * mean0(grad * plain))
    out_ref[...] = grad.T.reshape(12, 24, 128)

    send_left.wait_send()
    send_right.wait_send()
    send_dl.wait_send()
    send_dr.wait_send()
    wait(s1.at[pl.ds(0, 127)], send_sem.at[0])
    wait(s4.at[pl.ds(0, 127)], send_sem.at[7])
    wait(s2.at[pl.ds(0, 127)], send_sem.at[3])
    wait(s3.at[pl.ds(0, 127)], send_sem.at[4])

    @pl.when(jnp.logical_not(same))
    def _():
        wait(s2.at[0], send_sem.at[3])
        wait(s3.at[0], send_sem.at[4])


def local(pair, cotangent, norm_gain, gate_a, proj_a, gate_b, proj_b, mix_gain, out_gate, out_proj):
    def vmem(*shape):
        return pltpu.VMEM(shape, F32)

    return pl.pallas_call(
        kernel,
        out_shape=jax.ShapeDtypeStruct(pair.shape, F32),
        in_specs=[pl.BlockSpec(memory_space=pltpu.HBM)] * 10,
        out_specs=pl.BlockSpec(memory_space=pltpu.VMEM),
        scratch_shapes=[
            vmem(12, 24, 128), vmem(12, 24, 128), vmem(2, 1, 128), vmem(128, 640), vmem(128, 128),
            vmem(128, 1, 576), vmem(128, 1, 576),
            vmem(2, 96, 384), vmem(2, 96, 384), vmem(3, 192, 128),
            vmem(128, 1, 288), vmem(128, 1, 288),
            vmem(128, 1, 288), vmem(128, 1, 288),
            vmem(2, 96, 192),
            vmem(96, 384), vmem(96, 384), vmem(96, 384),
            vmem(3, 192, 128), vmem(2, 96, 384), vmem(96, 384),
            vmem(128, 1, 576), vmem(128, 1, 576),
            vmem(8, 128, 288), vmem(8, 288),
            pltpu.SemaphoreType.DMA((10,)), pltpu.SemaphoreType.DMA((8,)), pltpu.SemaphoreType.DMA((8,)),
        ],
        compiler_params=pltpu.CompilerParams(
            collective_id=0, has_side_effects=True, vmem_limit_bytes=VMEM),
    )(pair, cotangent, norm_gain.reshape(1, 128), gate_a, proj_a, gate_b, proj_b, mix_gain.reshape(1, 128),
      out_gate, out_proj)


def solution(mesh):
    placed = (P("row", "col", None), P("row", "col", None), P(), P(), P(), P(), P(), P(), P(), P())
    return jax.shard_map(
        local, mesh=mesh, in_specs=placed, out_specs=P("row", "col", None), check_vma=False)
```
